128 devices in a mesh: row: 16 (over y, x), col: 8 (over z, core).
Axes of the slice: x: 4, y: 4, z: 4, core: 2. Of those that a mesh axis runs over, the one named last changes fastest.
Arguments:
- out_grad: bfloat16 [131072, 256], P(('row', 'col')), may hold values from -6 to 6
- features: bfloat16 [131072, 256], P(('col', 'row')), may hold values from -6 to 6
- weight: bfloat16 [256, 256], replicated, may hold values from -0.375 to 0.375
- tiles: bfloat16 [16, 8, 384, 128, 128], P('row', 'col'), may hold values from -0.07470703 to 0.07470703
- row_block: int32 [16, 8, 384], P('row', 'col'), may hold values from 0 to 63
- col_block: int32 [16, 8, 384], P('row', 'col'), may hold values from 0 to 127
- live: int32 [16, 8, 384], P('row', 'col'), may hold values from 0 to 1, as said below
Outputs:
- input_grad: bfloat16 [131072, 256], P(('col', 'row'))
- weight_grad: float32 [256, 256], replicated
The draws below stay inside these ranges and needn't reach their ends.
Inputs may be any that keep to these rules, and one draw needn't show every extreme that they name: Each cell's slots of live hold between 48 and 384 ones, and in some cell all 384 slots are live.
All inputs are finite; a program needn't handle non-finite values.
Results may differ from the reference program's by a relative error of at most 0.0049.
Values may be sent and summed in bfloat16 or wider, within the bound.
No kernel may reach another device: no remote copies, remote signals or barrier semaphores. Data moves between devices by JAX's collectives and lax.ppermute only.
A program may use at most 256 MiB of HBM per device.

```python
import jax
import jax.numpy as jnp
from jax import lax

F = 256
BLOCK = 128
KT = 384
NODES = 131072
RBC = 64
CBC = 128
N_ROW = 16
N_COL = 8


def draw_live(key, part):
    key_count, key_full, key_order = jax.random.split(jax.random.fold_in(key, 17), 3)
    cells = N_ROW * N_COL
    counts = jax.random.randint(key_count, (cells,), KT // 8, KT + 1)
    full_cell = jax.random.randint(key_full, (), 0, cells)
    counts = jnp.where(jnp.arange(cells) == full_cell, KT, counts)
    scores = jax.random.randint(key_order, (cells, KT), 0, 1 << 20) * KT + jnp.arange(KT)[None, :]
    order = jnp.argsort(jnp.argsort(scores, axis=1, stable=True), axis=1, stable=True)
    return (order < counts[:, None]).astype(jnp.int32).reshape(N_ROW, N_COL, KT)


def set_ends(drawn, key, low, high):
    longest = drawn.shape.index(max(drawn.shape))
    spots = []
    for shift in (0, 1):
        where = [jax.random.randint(jax.random.fold_in(key, axis), (), 0, length) for axis, length in enumerate(drawn.shape)]
        where[longest] = (where[longest] + shift) % drawn.shape[longest]
        spots.append(tuple(where))
    return drawn.at[spots[0]].set(low).at[spots[1]].set(high)


def block_levels(key, shape, pieces, low, top_value):
    loudness, own = 1.0, jax.random.fold_in(key, 6)
    for axis_at, blocks in pieces:
        heights = jnp.exp(jax.random.uniform(jax.random.fold_in(own, axis_at), (blocks,), jnp.float32, low / len(pieces), top_value / len(pieces)))
        loudness = loudness * jnp.repeat(heights, shape[axis_at] // blocks).reshape([-1 if axis == axis_at else 1 for axis in range(len(shape))])
    return loudness


def normal_values(stream_key, dims, deviation, reach, pieces=(), held_as=jnp.bfloat16):
    values = jax.random.normal(stream_key, dims, jnp.float32) * deviation
    if len(pieces) > 0:
        values = block_levels(stream_key, dims, pieces, -0.22, 0.18) * values
    return jnp.clip(values, min=-reach, max=reach).astype(held_as)


def setup_inputs(seed: int = 0) -> dict:
    seeds = jax.random.split(jax.random.key(seed), 8)
    return {
        "out_grad": normal_values(seeds[0], (NODES, F), 1.0, 6.0, ((0, 128),)),
        "features": normal_values(seeds[1], (NODES, F), 1.0, 6.0, ((0, 128),)),
        "weight": normal_values(seeds[2], (F, F), F ** -0.5, 0.375),
        "tiles": normal_values(seeds[3], (N_ROW, N_COL, KT, BLOCK, BLOCK), 0.0125, 0.07470703, ((0, 16), (1, 8))),
        "row_block": set_ends(jax.random.randint(seeds[4], (N_ROW, N_COL, KT), 0, RBC), jax.random.fold_in(seeds[4], 1), 0, RBC - 1).astype(jnp.int32),
        "col_block": set_ends(jax.random.randint(seeds[5], (N_ROW, N_COL, KT), 0, CBC), jax.random.fold_in(seeds[5], 1), 0, CBC - 1).astype(jnp.int32),
        "live": draw_live(jax.random.fold_in(seeds[7], 71), 0),
    }


def reference(out_grad, features, weight, tiles, row_block, col_block, live):
    cells = N_ROW * N_COL
    block_count = NODES // BLOCK
    grad_blocks = out_grad.reshape(block_count, BLOCK, F)
    tile_cells = tiles.reshape(cells, KT, BLOCK, BLOCK)
    row_cells = row_block.reshape(cells, KT)
    col_cells = col_block.reshape(cells, KT)
    live_cells = live.reshape(cells, KT)
    cell_ids = jnp.arange(cells, dtype=jnp.int32)

    def add_cell(carry, inputs):
        tile_set, row_ids, col_ids, live_ids, cell_index = inputs
        group_row = cell_index // N_COL
        group_col = cell_index % N_COL
        global_rows = (group_row * RBC + row_ids).astype(jnp.int32)
        global_cols = (group_col * CBC + col_ids).astype(jnp.int32)
        panels = grad_blocks[global_rows]
        contrib = jnp.einsum("kij,kif->kjf", tile_set.astype(jnp.float32), panels.astype(jnp.float32))
        contrib = contrib * live_ids.astype(jnp.float32)[:, None, None]
        carry = carry + jax.ops.segment_sum(contrib, global_cols, num_segments=block_count)
        return carry, None

    start = jnp.zeros((block_count, BLOCK, F), jnp.float32)
    summed, _ = lax.scan(add_cell, start, (tile_cells, row_cells, col_cells, live_cells, cell_ids))
    column_grad = summed.reshape(NODES, F).astype(jnp.bfloat16)
    input_grad = jnp.dot(column_grad, weight.T, preferred_element_type=jnp.float32).astype(jnp.bfloat16)
    weight_grad = jnp.dot(features.T, column_grad, preferred_element_type=jnp.float32) * (NODES ** -0.5)
    return input_grad, weight_grad
```

```python
import functools

import jax
import jax.numpy as jnp
from jax import lax
from jax.experimental import pallas as pl
from jax.experimental.pallas import tpu as pltpu
from jax.sharding import PartitionSpec as P

F32, BF16 = jnp.float32, jnp.bfloat16
B = 128
NY = NX = NZ = 4
DUMMY = 128
CHUNK = 32
SLOTS = 4

XP = [[(y * NX + x, y * NX + (x + s) % NX) for y in range(NY) for x in range(NX)] for s in range(4)]
YP = [[(y * NX + x, (y + s) % NY * NX + x) for y in range(NY) for x in range(NX)] for s in range(4)]
ZP = [[(z * 2 + c, (z + s) % NZ * 2 + c) for z in range(NZ) for c in range(2)] for s in range(4)]
CP = [(z * 2 + c, z * 2 + 1 - c) for z in range(NZ) for c in range(2)]


def xperm(v, s):
    return lax.ppermute(v, "row", XP[s])


def yperm(v, s):
    return lax.ppermute(v, "row", YP[s])


def zperm(v, s):
    return lax.ppermute(v, "col", ZP[s])


def cperm(v):
    return lax.ppermute(v, "col", CP)


def panels_kernel(x_ref, lo_ref, hi_ref):
    for b in range(8):
        block = x_ref[b * B : (b + 1) * B, :].astype(F32)
        lo_ref[b] = block[:, :B].T.astype(BF16)
        hi_ref[b] = block[:, B:].T.astype(BF16)


def panels(out_grad):
    shape = jax.ShapeDtypeStruct((8, B, B), BF16)
    return pl.pallas_call(panels_kernel, out_shape=(shape, shape), name="panels")(out_grad)


OUT_BLOCKS = (16, 16, 16, 8, 8) * 2


def tile_kernel(rmap, cmap, tiles, *refs):
    xs = refs[:8]
    outs = refs[8:18]
    xbuf, tbuf, acc, stage, tsem, xsem, osem = refs[18:]
    slots = tiles.shape[0] // CHUNK

    def tile_copy(c, slot):
        return pltpu.make_async_copy(tiles.at[pl.ds(c * CHUNK, CHUNK)], tbuf.at[slot], tsem.at[slot])

    x_copies = [pltpu.make_async_copy(xs[i], xbuf.at[pl.ds(i * 8, 8)], xsem.at[i]) for i in range(8)]
    for copy in x_copies:
        copy.start()
    for c in range(SLOTS - 1):
        tile_copy(c, c).start()
    acc[...] = jnp.zeros_like(acc)
    for copy in x_copies:
        copy.wait()

    def chunk(c, carry):
        slot = lax.rem(c, SLOTS)
        tile_copy(c, slot).wait()

        @pl.when(c + SLOTS - 1 < slots)
        def _():
            tile_copy(c + SLOTS - 1, lax.rem(c + SLOTS - 1, SLOTS)).start()

        products = [
            jnp.dot(xbuf[rmap[c * CHUNK + u]], tbuf[slot, u], preferred_element_type=F32) for u in range(CHUNK)
        ]
        for u in range(CHUNK):
            acc[cmap[c * CHUNK + u]] += products[u]
        return carry

    lax.fori_loop(0, slots, chunk, 0)
    at = 0
    copies = []
    for i, n in enumerate(OUT_BLOCKS):
        stage[pl.ds(at, n)] = acc[pl.ds(at, n)].astype(BF16)
        copy = pltpu.make_async_copy(stage.at[pl.ds(at, n)], outs[i], osem.at[i])
        copy.start()
        copies.append(copy)
        at += n
    for copy in copies:
        copy.wait()


def tile_products(rmap, cmap, tiles, xs):
    hbm = pl.BlockSpec(memory_space=pl.ANY)
    return pl.pallas_call(
        tile_kernel,
        grid_spec=pltpu.PrefetchScalarGridSpec(
            num_scalar_prefetch=2,
            grid=(1,),
            in_specs=[hbm] * 9,
            out_specs=[hbm] * 10,
            scratch_shapes=[
                pltpu.VMEM((64, B, B), BF16),
                pltpu.VMEM((SLOTS, CHUNK, B, B), BF16),
                pltpu.VMEM((DUMMY + 1, B, B), F32),
                pltpu.VMEM((128, B, B), BF16),
                pltpu.SemaphoreType.DMA((SLOTS,)),
                pltpu.SemaphoreType.DMA((8,)),
                pltpu.SemaphoreType.DMA((10,)),
            ],
        ),
        out_shape=[jax.ShapeDtypeStruct((n, B, B), BF16) for n in OUT_BLOCKS],
        compiler_params=pltpu.CompilerParams(vmem_limit_bytes=24 * 2**20),
        name="tile_products",
    )(rmap, cmap, tiles, *xs)


def finish_kernel(*refs):
    parts, (feat, weight, ig, wg) = refs[:16], refs[16:]
    total = jnp.zeros((256, 256), F32)
    for b in range(8):
        half, i = b // 4, b % 4
        cols = []
        for h in range(2):
            four = parts[(h * 2 + half) * 4 : (h * 2 + half) * 4 + 4]
            s = four[0][i] + four[1][i].astype(F32)
            s = s + four[2][i].astype(F32) + four[3][i].astype(F32)
            cols.append(s)
        cg = jnp.concatenate(cols, axis=0).astype(BF16)
        rows = slice(b * B, (b + 1) * B)
        ig[rows, :] = lax.dot_general(
            cg, weight[...], (((0,), (1,)), ((), ())), preferred_element_type=F32
        ).astype(BF16)
        total = total + jnp.dot(cg, feat[rows, :], preferred_element_type=F32)
    wg[...] = total


def finish(parts, features, weight):
    return pl.pallas_call(
        finish_kernel,
        out_shape=(
            jax.ShapeDtypeStruct((1024, 256), BF16),
            jax.ShapeDtypeStruct((256, 256), F32),
        ),
        compiler_params=pltpu.CompilerParams(vmem_limit_bytes=16 * 2**20),
        name="finish",
    )(*parts, features, weight)


def gather(own):
    one, three, two = zperm(own, 1), zperm(own, 3), zperm(own, 2)
    return [own, cperm(own), three, cperm(three), two, cperm(two), one, cperm(one)]


def f32(v):
    return v.astype(F32)


def reduce_part(part, first, second):
    own, up, um, vp, vm = part
    rp, rm = first(up, 1), first(um, 3)
    sp = first((f32(vp) + f32(rp[:8])).astype(BF16), 1)
    sm = first((f32(vm) + f32(rm[:8])).astype(BF16), 3)
    low = f32(own[:8]) + f32(rm[8:]) + f32(sp)
    high = f32(own[8:]) + f32(rp[8:]) + f32(sm)
    t1, t2, t3 = low[4:].astype(BF16), high[:4].astype(BF16), high[4:].astype(BF16)
    return [low[:4], second(t1, 1), second(t2, 2), second(t3, 3)]


def rel(stack, at):
    n = stack.shape[0] // 4
    return lax.dynamic_slice_in_dim(stack, (at % 4) * n, n, 0)


def all_sum(v, z, core):
    half = v.shape[0] // 2
    mine = lax.dynamic_slice_in_dim(v, core * half, half, 0)
    other = lax.dynamic_slice_in_dim(v, (1 - core) * half, half, 0)
    v = mine + cperm(other)
    v = (rel(v, z) + zperm(rel(v, z + 2), 2)) + (zperm(rel(v, z + 1), 1) + zperm(rel(v, z + 3), 3))
    v = (v + xperm(v, 2)) + (xperm(v, 1) + xperm(v, 3))
    v = (v + yperm(v, 2)) + (yperm(v, 1) + yperm(v, 3))
    four = jnp.concatenate([v, zperm(v, 3), zperm(v, 2), zperm(v, 1)] * 2, axis=0)
    n = v.shape[0]
    v = lax.dynamic_slice_in_dim(four, ((4 - z) % 4) * n, 4 * n, 0)
    two = jnp.concatenate([v, cperm(v)] * 2, axis=0)
    return lax.dynamic_slice_in_dim(two, core * half, 2 * half, 0)


def local(out_grad, features, weight, tiles, row_block, col_block, live):
    row, col = lax.axis_index("row"), lax.axis_index("col")
    y, x, z, core = row // NX, row % NX, col // 2, col % 2
    rb, cb, on = row_block[0, 0], col_block[0, 0], live[0, 0]
    src = rb // 8
    rmap = (((src // 2 - z) % NZ) * 2 + (src % 2 + core) % 2) * 8 + rb % 8
    dest, b = cb // 8, cb % 8
    rx, ry = (dest % NX - x) % NX, (dest // NX - y) % NY
    in_first = b < 4
    major, minor = jnp.where(in_first, rx, ry), jnp.where(in_first, ry, rx)
    low = minor < 2
    start = jnp.where(
        major == 0,
        minor * 4,
        jnp.where(
            major == 1,
            jnp.where(low, 48 + minor * 4, 24 + (minor - 2) * 4),
            jnp.where(
                major == 2,
                jnp.where(low, 16 + minor * 4, 32 + (minor - 2) * 4),
                jnp.where(low, 40 + minor * 4, 56 + (minor - 2) * 4),
            ),
        ),
    )
    cmap = jnp.where(on > 0, start + b % 4 + jnp.where(in_first, 0, 64), DUMMY)

    halves = panels(out_grad)
    parts = []
    for own in halves:
        outs = tile_products(rmap, cmap, tiles[0, 0], gather(own))
        parts += reduce_part(outs[:5], xperm, yperm)
        parts += reduce_part(outs[5:], yperm, xperm)
    input_grad, wg = finish(parts, features, weight)
    wg = all_sum(wg, z, core)
    nodes = 1024 * 128
    return input_grad, wg.T * nodes ** (-0.5)


def solution(mesh):
    return jax.shard_map(
        local,
        mesh=mesh,
        in_specs=(
            P(("row", "col"), None),
            P(("col", "row"), None),
            P(),
            P("row", "col", None, None, None),
            P("row", "col", None),
            P("row", "col", None),
            P("row", "col", None),
        ),
        out_specs=(P(("col", "row"), None), P()),
        check_vma=False,
    )
```

```python
import functools

import jax
import jax.numpy as jnp
from jax import lax
from jax.experimental import pallas as pl
from jax.experimental.pallas import tpu as pltpu
from jax.sharding import PartitionSpec as P

F32, BF16 = jnp.float32, jnp.bfloat16
B = 128
NY = NX = NZ = 4
HALF = 64
UNROLL = 16
FW = 256
KT = 384
VMEM = pl.BlockSpec(memory_space=pltpu.VMEM)
SMEM = pl.BlockSpec(memory_space=pltpu.SMEM)
ANY = pl.BlockSpec(memory_space=pl.ANY)


def params(mib):
    return pltpu.CompilerParams(vmem_limit_bytes=mib * 2**20)


def shaped(shape, dtype=BF16):
    return jax.ShapeDtypeStruct(shape, dtype)


XP = [[(y * NX + x, y * NX + (x + s) % NX) for y in range(NY) for x in range(NX)] for s in range(4)]
YP = [[(y * NX + x, (y + s) % NY * NX + x) for y in range(NY) for x in range(NX)] for s in range(4)]
ZP = [[(z * 2 + c, (z + s) % NZ * 2 + c) for z in range(NZ) for c in range(2)] for s in range(4)]
CP = [(z * 2 + c, z * 2 + 1 - c) for z in range(NZ) for c in range(2)]


def xperm(v, s):
    return lax.ppermute(v, "row", XP[s])


def yperm(v, s):
    return lax.ppermute(v, "row", YP[s])


def zperm(v, s):
    return lax.ppermute(v, "col", ZP[s])


def cperm(v):
    return lax.ppermute(v, "col", CP)


def panels_kernel(x_ref, out_ref):
    for b in range(8):
        out_ref[b] = x_ref[b * B : (b + 1) * B, :].astype(F32).T.astype(BF16)


def panels(out_grad):
    return pl.pallas_call(
        panels_kernel,
        out_shape=shaped((8, FW, B)),
        compiler_params=params(6),
        name="panels",
    )(out_grad)


def codes_kernel(at, row_block, col_block, live, after, code):
    y, x, z, core = (at[i] for i in range(4))
    rb, cb = row_block[...], col_block[...]
    src = rb >> 3
    panel = (((src + core) & 1) << 5) + ((((src >> 1) - z) & 3) << 3) + (rb & 7)
    dest, b = cb >> 3, cb & 7
    rx, ry = (dest - x) & 3, ((dest >> 2) - y) & 3
    in_first = b < 4
    major, minor = jnp.where(in_first, rx, ry), jnp.where(in_first, ry, rx)
    low = minor < 2
    kept = (major == 0) | (low & (major == 1)) | ((minor >= 2) & (major == 3))
    kept_at = minor * 4 + jnp.where(major == 0, 0, 16)
    far = minor * 4 + jnp.where(low, 0, 8)
    near = minor * 4 + jnp.where(major == 1, 0, 24)
    sent_at = jnp.where(major == 2, far, near)
    target = jnp.where(kept, kept_at, sent_at) + (b & 3) + jnp.where(in_first, 0, 32)
    group = jnp.where(live[...] > 0, jnp.where(kept, 1, 0), 2)
    tile = lax.broadcasted_iota(jnp.int32, rb.shape, 2)
    code[...] = (group << 23) + (target << 15) + (panel << 9) + tile


def codes(at, row_block, col_block, live, after):
    return pl.pallas_call(
        codes_kernel,
        in_specs=[SMEM] + [VMEM] * 3 + [ANY],
        out_shape=shaped((1, 1, KT), jnp.int32),
        compiler_params=params(4),
        name="codes",
    )(at, row_block, col_block, live, after)


def again_kernel(a, b, c, *refs):
    for source, target in zip((a, b, c), refs[-3:]):
        target[...] = source[...]


def again(arrays, after):
    return pl.pallas_call(
        again_kernel,
        in_specs=[VMEM] * 3 + [ANY] * len(after),
        out_shape=[shaped(a.shape) for a in arrays],
        compiler_params=params(6),
        name="again",
    )(*arrays, *after)


def stage_kernel(tiles, code, place, after, held, first, second, count, masks, sem):
    copy = pltpu.make_async_copy(tiles, held, sem)
    copy.start()
    for i in range(2):
        masks[i] = jnp.full((8, 256), place[i], jnp.int32)

    def step(g, counts):
        a, b = counts
        for u in range(8):
            v = code[0, 0, g * 8 + u]
            group = v >> 23
            entry = v & (2**23 - 1)
            first[a] = entry
            second[b] = entry
            a = a + (group == 0).astype(jnp.int32)
            b = b + (group & 1)
        return a, b

    a, b = lax.fori_loop(0, KT // 8, step, (jnp.int32(0), jnp.int32(0)))
    for u in range(UNROLL):
        first[a + u] = HALF * 2**15
        second[b + u] = HALF * 2**15
    count[0] = (a + UNROLL - 1) // UNROLL
    count[1] = (b + UNROLL - 1) // UNROLL
    copy.wait()


def stage(tiles, code, place, after):
    return pl.pallas_call(
        stage_kernel,
        in_specs=[ANY, SMEM, SMEM, ANY],
        out_specs=[VMEM, SMEM, SMEM, SMEM, VMEM],
        out_shape=[
            shaped((KT, B, B)),
            shaped((KT + UNROLL,), jnp.int32),
            shaped((KT + UNROLL,), jnp.int32),
            shaped((2,), jnp.int32),
            shaped((2, 8, 256), jnp.int32),
        ],
        scratch_shapes=[pltpu.SemaphoreType.DMA(())],
        compiler_params=params(16),
        name="stage",
    )(tiles, code, place, after)


def products(which, entries, count, tiles, x, acc):
    acc[...] = jnp.zeros_like(acc)

    def step(g, carry):
        targets, values = [], []
        for u in range(UNROLL):
            v = entries[g * UNROLL + u]
            c = v >> 15
            r = (v >> 9) & 63
            k = v & 511
            targets.append(c)
            values.append(jnp.dot(x[r], tiles[k], preferred_element_type=F32))
        for c, value in zip(targets, values):
            acc[c] += value
        return carry

    lax.fori_loop(0, count[which], step, 0)


def write_out(acc, outs):
    at = 0
    for out in outs:
        n = out.shape[0]
        out[...] = acc[pl.ds(at, n)].astype(BF16)
        at += n


SEND = (16, 16) * 2
KEEP = (16, 8, 8) * 2


def send_kernel(entries, count, tiles, *refs):
    xs, x, outs, acc = refs[:8], refs[8], refs[9:13], refs[13]
    for i in range(8):
        x[i * 8 : (i + 1) * 8] = xs[i][...]
    products(0, entries, count, tiles, x, acc)
    write_out(acc, outs)


def keep_kernel(entries, count, tiles, x, *refs):
    outs, acc = refs[:6], refs[6]
    products(1, entries, count, tiles, x, acc)
    write_out(acc, outs)


ACC = pltpu.VMEM((HALF + 1, FW, B), F32)


def send_products(entries, count, tiles, xs):
    out = pl.pallas_call(
        send_kernel,
        in_specs=[SMEM, SMEM, VMEM] + [VMEM] * 8,
        out_specs=[VMEM] * 5,
        out_shape=[shaped((n, FW, B)) for n in (64,) + SEND],
        scratch_shapes=[ACC],
        compiler_params=params(12),
        name="send_products",
    )(entries, count, tiles, *xs)
    return out[0], out[1:]


def keep_products(entries, count, tiles, x):
    return pl.pallas_call(
        keep_kernel,
        in_specs=[SMEM, SMEM, VMEM, VMEM],
        out_specs=[VMEM] * 6,
        out_shape=[shaped((n, FW, B)) for n in KEEP],
        scratch_shapes=[ACC],
        compiler_params=params(12),
        name="keep_products",
    )(entries, count, tiles, x)


def middle_kernel(*refs):
    received, outs = refs[:10], refs[10:]
    for half in range(2):
        own, rp, rm, sp, sm = received[half * 5 : half * 5 + 5]
        for place in range(4):
            out = outs[half * 4 + place]
            for i in range(4):
                n = place * 4 + i
                if place < 2:
                    s = own[n].astype(F32) + rm[8 + n].astype(F32) + sp[n].astype(F32)
                else:
                    s = own[n].astype(F32) + rp[n].astype(F32) + sm[n - 8].astype(F32)
                out[i] = s.astype(out.dtype)


def middle(received):
    dtypes = (F32, BF16, BF16, BF16) * 2
    return pl.pallas_call(
        middle_kernel,
        out_shape=[shaped((4, FW, B), t) for t in dtypes],
        compiler_params=params(14),
        name="middle",
    )(*received)


def finish_kernel(*refs):
    parts, (feat, weight, ig, wg) = refs[:8], refs[8:]
    total = jnp.zeros((FW, 256), F32)
    for b in range(8):
        four = parts[b // 4 * 4 : b // 4 * 4 + 4]
        i = b % 4
        rows = slice(b * B, (b + 1) * B)
        s = four[0][i] + four[1][i].astype(F32)
        cg = (s + four[2][i].astype(F32) + four[3][i].astype(F32)).astype(BF16)
        total = total + jnp.dot(cg, feat[rows, :], preferred_element_type=F32)
        ig[rows, :] = lax.dot_general(
            cg, weight[...], (((0,), (1,)), ((), ())), preferred_element_type=F32
        ).astype(BF16)
    wg[...] = total


def finish(parts, features, weight):
    return pl.pallas_call(
        finish_kernel,
        out_shape=[shaped((8 * B, 256)), shaped((FW, 256), F32)],
        compiler_params=params(10),
        name="finish",
    )(*parts, features, weight)


def f32(v):
    return v.astype(F32)


def split(v, at):
    n = v.shape[0] // 2
    low, high = v[:n], v[n:]
    return jnp.where(at == 0, low, high), jnp.where(at == 0, high, low)


def unite(mine, other, at):
    return jnp.concatenate([jnp.where(at == 0, mine, other), jnp.where(at == 0, other, mine)], axis=0)


def all_sum(v, masks):
    core, z = masks[0, :1], masks[1, :1]
    mine, other = split(v, core)
    v = mine + lax.ppermute(other, "col", CP)
    n = v.shape[0] // 4
    pieces = [v[i * n : (i + 1) * n] for i in range(4)]

    def piece(k):
        at = (z + k) & 3
        return jnp.where(at < 2, jnp.where(at == 0, pieces[0], pieces[1]), jnp.where(at == 2, pieces[2], pieces[3]))

    v = (piece(0) + zperm(piece(2), 2)) + (zperm(piece(1), 1) + zperm(piece(3), 3))
    v = (v + xperm(v, 2)) + (xperm(v, 1) + xperm(v, 3))
    v = (v + yperm(v, 2)) + (yperm(v, 1) + yperm(v, 3))
    four = [v, zperm(v, 3), zperm(v, 2), zperm(v, 1)]

    def placed(i):
        at = (i - z) & 3
        return jnp.where(at < 2, jnp.where(at == 0, four[0], four[1]), jnp.where(at == 2, four[2], four[3]))

    v = jnp.concatenate([placed(i) for i in range(4)], axis=0)
    return unite(v, cperm(v), core)


def local(out_grad, features, weight, tiles, row_block, col_block, live):
    row, col = lax.axis_index("row"), lax.axis_index("col")
    y, x, z, core = row // NX, row % NX, col // 2, col % 2
    own = panels(out_grad)
    own_turned = cperm(own)
    one, three, two = zperm(own, 1), zperm(own, 3), zperm(own, 2)
    at = jnp.stack([y, x, z, core]).astype(jnp.int32)
    place = jnp.stack([core, z]).astype(jnp.int32)
    code = codes(at, row_block, col_block, live, own)
    held, first, second, count, masks = stage(tiles[0, 0], code, place, own)
    one, three, two = again((one, three, two), [held])
    xs = [own, three, two, one, own_turned, cperm(three), cperm(two), cperm(one)]

    ways = ((xperm, 1), (xperm, 3), (yperm, 1), (yperm, 3))

    def swap(buffers):
        return [perm(v, s) for v, (perm, s) in zip(buffers, ways)]

    stacked, send = send_products(first, count, held, xs)
    got = swap(send)
    keep = keep_products(second, count, held, stacked)
    turned = [keep[1], keep[2], keep[4], keep[5]]
    more = swap([(f32(v) + f32(g[:8])).astype(BF16) for v, g in zip(turned, got)])
    received = [keep[0], *got[:2], *more[:2], keep[3], *got[2:], *more[2:]]
    sums = middle(received)
    parts = [sums[0]] + [yperm(sums[k], k) for k in (1, 2, 3)]
    parts += [sums[4]] + [xperm(sums[4 + k], k) for k in (1, 2, 3)]
    input_grad, wg = finish(parts, features, weight)
    nodes = 1024 * 128
    return input_grad, all_sum(wg, masks).T * nodes ** (-0.5)


def solution(mesh):
    return jax.shard_map(
        local,
        mesh=mesh,
        in_specs=(
            P(("row", "col"), None),
            P(("col", "row"), None),
            P(),
            P("row", "col", None, None, None),
            P("row", "col", None),
            P("row", "col", None),
            P("row", "col", None),
        ),
        out_specs=(P(("col", "row"), None), P()),
        check_vma=False,
    )
```

```python
import functools

import jax
import jax.numpy as jnp
from jax import lax
from jax.experimental import pallas as pl
from jax.experimental.pallas import tpu as pltpu
from jax.sharding import PartitionSpec as P

F32, BF16 = jnp.float32, jnp.bfloat16
B = 128
NY = NX = NZ = 4
HALF = 64
UNROLL = 32
KT = 384
VMEM = pl.BlockSpec(memory_space=pltpu.VMEM)
SMEM = pl.BlockSpec(memory_space=pltpu.SMEM)
ANY = pl.BlockSpec(memory_space=pl.ANY)


def params(mib):
    return pltpu.CompilerParams(vmem_limit_bytes=mib * 2**20)


def shaped(shape, dtype=BF16):
    return jax.ShapeDtypeStruct(shape, dtype)


XP = [[(y * NX + x, y * NX + (x + s) % NX) for y in range(NY) for x in range(NX)] for s in range(4)]
YP = [[(y * NX + x, (y + s) % NY * NX + x) for y in range(NY) for x in range(NX)] for s in range(4)]
ZP = [[(z * 2 + c, (z + s) % NZ * 2 + c) for z in range(NZ) for c in range(2)] for s in range(4)]
CP = [(z * 2 + c, z * 2 + 1 - c) for z in range(NZ) for c in range(2)]


def xperm(v, s):
    return lax.ppermute(v, "row", XP[s])


def yperm(v, s):
    return lax.ppermute(v, "row", YP[s])


def zperm(v, s):
    return lax.ppermute(v, "col", ZP[s])


def cperm(v):
    return lax.ppermute(v, "col", CP)


def transposed(x_ref, out_ref):
    for b in range(8):
        out_ref[b] = x_ref[b * B : (b + 1) * B, :].astype(F32).T.astype(BF16)


def low_kernel(x_ref, out_ref):
    transposed(x_ref, out_ref)


def low_panels(out_grad):
    return pl.pallas_call(
        low_kernel,
        grid=(1,),
        in_specs=[pl.BlockSpec((8 * B, B), lambda i: (0, 0))],
        out_specs=pl.BlockSpec((8, B, B), lambda i: (0, 0, 0)),
        out_shape=shaped((8, B, B)),
        compiler_params=params(4),
        name="low_panels",
    )(out_grad)


def codes_kernel(at, row_block, col_block, live, after, code):
    y, x, z, core = (at[i] for i in range(4))
    rb, cb = row_block[...], col_block[...]
    src = rb >> 3
    panel = (((src + core) & 1) << 5) + ((((src >> 1) - z) & 3) << 3) + (rb & 7)
    dest, b = cb >> 3, cb & 7
    rx, ry = (dest - x) & 3, ((dest >> 2) - y) & 3
    in_first = b < 4
    major, minor = jnp.where(in_first, rx, ry), jnp.where(in_first, ry, rx)
    low = minor < 2
    kept = (major == 0) | (low & (major == 1)) | ((minor >= 2) & (major == 3))
    kept_at = minor * 4 + jnp.where(major == 0, 0, 16)
    far = minor * 4 + jnp.where(low, 0, 8)
    near = minor * 4 + jnp.where(major == 1, 0, 24)
    sent_at = jnp.where(major == 2, far, near)
    target = jnp.where(kept, kept_at, sent_at) + (b & 3) + jnp.where(in_first, 0, 32)
    group = jnp.where(live[...] > 0, jnp.where(kept, 1, 0), 2)
    tile = lax.broadcasted_iota(jnp.int32, rb.shape, 2)
    code[...] = (group << 23) + (target << 15) + (panel << 9) + tile


def codes(at, row_block, col_block, live, after):
    return pl.pallas_call(
        codes_kernel,
        in_specs=[SMEM] + [VMEM] * 3 + [ANY],
        out_shape=shaped((1, 1, KT), jnp.int32),
        compiler_params=params(4),
        name="codes",
    )(at, row_block, col_block, live, after)


def high_kernel(x_ref, *refs):
    transposed(x_ref, refs[-1])


def high_panels(out_grad, after):
    return pl.pallas_call(
        high_kernel,
        grid=(1,),
        in_specs=[pl.BlockSpec((8 * B, B), lambda i: (0, 1))] + [ANY] * len(after),
        out_specs=pl.BlockSpec((8, B, B), lambda i: (0, 0, 0)),
        out_shape=shaped((8, B, B)),
        compiler_params=params(4),
        name="high_panels",
    )(out_grad, *after)


def again_kernel(a, b, c, *refs):
    for source, target in zip((a, b, c), refs[-3:]):
        target[...] = source[...]


def again(arrays, after):
    return pl.pallas_call(
        again_kernel,
        in_specs=[VMEM] * 3 + [ANY],
        out_shape=[shaped(a.shape) for a in arrays],
        compiler_params=params(6),
        name="again",
    )(*arrays, after)


def stage_kernel(tiles, code, place, after, held, first, second, count, masks, sem):
    copy = pltpu.make_async_copy(tiles, held, sem)
    copy.start()
    for i in range(2):
        masks[i] = jnp.full((8, 256), place[2 + i], jnp.int32)

    def step(g, counts):
        a, b = counts
        for u in range(8):
            v = code[0, 0, g * 8 + u]
            group = v >> 23
            entry = v & (2**23 - 1)
            first[a] = entry
            second[b] = entry
            a = a + (group == 0).astype(jnp.int32)
            b = b + (group & 1)
        return a, b

    a, b = lax.fori_loop(0, KT // 8, step, (jnp.int32(0), jnp.int32(0)))
    for u in range(UNROLL):
        first[a + u] = HALF * 2**15
        second[b + u] = HALF * 2**15
    count[0] = (a + UNROLL - 1) // UNROLL
    count[1] = (b + UNROLL - 1) // UNROLL
    copy.wait()


def stage(tiles, code, place, after):
    return pl.pallas_call(
        stage_kernel,
        in_specs=[ANY, SMEM, SMEM, ANY],
        out_specs=[VMEM, SMEM, SMEM, SMEM, VMEM],
        out_shape=[
            shaped((KT, B, B)),
            shaped((KT + UNROLL,), jnp.int32),
            shaped((KT + UNROLL,), jnp.int32),
            shaped((2,), jnp.int32),
            shaped((2, 8, 256), jnp.int32),
        ],
        scratch_shapes=[pltpu.SemaphoreType.DMA(())],
        compiler_params=params(16),
        name="stage",
    )(tiles, code, place, after)


def products(which, entries, count, tiles, x, acc):
    acc[...] = jnp.zeros_like(acc)

    def step(g, carry):
        targets, values = [], []
        for u in range(UNROLL):
            v = entries[g * UNROLL + u]
            c = v >> 15
            r = (v >> 9) & 63
            k = v & 511
            targets.append(c)
            values.append(jnp.dot(x[r], tiles[k], preferred_element_type=F32))
        for c, value in zip(targets, values):
            acc[c] += value
        return carry

    lax.fori_loop(0, count[which], step, 0)


def write_out(acc, outs):
    at = 0
    for out in outs:
        n = out.shape[0]
        out[...] = acc[pl.ds(at, n)].astype(BF16)
        at += n


SEND = (16, 16) * 2
KEEP = (16, 8, 8) * 2


def send_kernel(entries, count, tiles, *refs):
    xs, x, outs, acc = refs[:8], refs[8], refs[9:13], refs[13]
    for i in range(8):
        x[i * 8 : (i + 1) * 8] = xs[i][...]
    products(0, entries, count, tiles, x, acc)
    write_out(acc, outs)


def keep_kernel(entries, count, tiles, x, *refs):
    outs, acc = refs[:6], refs[6]
    products(1, entries, count, tiles, x, acc)
    write_out(acc, outs)


ACC = pltpu.VMEM((HALF + 1, B, B), F32)


def send_products(entries, count, tiles, xs):
    out = pl.pallas_call(
        send_kernel,
        in_specs=[SMEM, SMEM, VMEM] + [VMEM] * 8,
        out_specs=[VMEM] * 5,
        out_shape=[shaped((n, B, B)) for n in (64,) + SEND],
        scratch_shapes=[ACC],
        compiler_params=params(12),
        name="send_products",
    )(entries, count, tiles, *xs)
    return out[0], out[1:]


def keep_products(entries, count, tiles, x):
    return pl.pallas_call(
        keep_kernel,
        in_specs=[SMEM, SMEM, VMEM, VMEM],
        out_specs=[VMEM] * 6,
        out_shape=[shaped((n, B, B)) for n in KEEP],
        scratch_shapes=[ACC],
        compiler_params=params(12),
        name="keep_products",
    )(entries, count, tiles, x)


def join_kernel(*refs):
    ins, outs = refs[:12], refs[12:]
    for i in range(4):
        kept, got, sent = ins[i * 3 : i * 3 + 3]
        outs[i][:8] = (kept[...].astype(F32) + got[:8].astype(F32)).astype(BF16)
        outs[i][8:] = sent[...]


def join(keep, received, send):
    ins = []
    for kept, got, sent in zip(keep, received, send):
        ins += [kept, got, sent]
    return pl.pallas_call(
        join_kernel,
        out_shape=[shaped((24, B, B))] * 4,
        compiler_params=params(12),
        name="join",
    )(*ins)


def middle_kernel(*refs):
    received = refs[:10]
    last = len(refs) > 18
    before, outs = (refs[10:18], refs[18:]) if last else ((), refs[10:])
    at, skip = (4, 8) if last else (0, 0)
    if last:
        for i in range(8):
            outs[i][:4] = before[i][...]
    for half in range(2):
        own, rp, rm, sp, sm = received[half * 5 : half * 5 + 5]
        for place in range(4):
            out = outs[half * 4 + place]
            for i in range(4):
                n = place * 4 + i
                if place < 2:
                    s = own[n].astype(F32) + rm[skip + 8 + n].astype(F32) + sp[n].astype(F32)
                else:
                    s = own[n].astype(F32) + rp[skip + n].astype(F32) + sm[n - 8].astype(F32)
                out[at + i] = s.astype(out.dtype)


def middle(received, before):
    n = 8 if before else 4
    dtypes = (F32, BF16, BF16, BF16) * 2
    return pl.pallas_call(
        middle_kernel,
        out_shape=[shaped((n, B, B), t) for t in dtypes],
        compiler_params=params(14),
        name="middle",
    )(*received, *before)


def column_grad(parts, b):
    four = parts[b // 4 * 4 : b // 4 * 4 + 4]
    halves = []
    for h in range(2):
        i = h * 4 + b % 4
        s = four[0][i] + four[1][i].astype(F32)
        halves.append(s + four[2][i].astype(F32) + four[3][i].astype(F32))
    return jnp.concatenate(halves, axis=0).astype(BF16)


def weight_kernel(*refs):
    parts, (feat, wg) = refs[:8], refs[8:]
    total = jnp.zeros((256, 256), F32)
    for b in range(8):
        total = total + jnp.dot(
            column_grad(parts, b), feat[b * B : (b + 1) * B, :], preferred_element_type=F32
        )
    wg[...] = total.T


def input_kernel(*refs):
    parts, (weight, ig) = refs[:8], refs[8:]
    for b in range(8):
        ig[b * B : (b + 1) * B, :] = lax.dot_general(
            column_grad(parts, b), weight[...], (((0,), (1,)), ((), ())), preferred_element_type=F32
        ).astype(BF16)


def weight_share(parts, features):
    return pl.pallas_call(
        weight_kernel,
        out_shape=shaped((256, 256), F32),
        compiler_params=params(10),
        name="weight_share",
    )(*parts, features)


def input_share(parts, weight):
    return pl.pallas_call(
        input_kernel,
        out_shape=shaped((8 * B, 256)),
        compiler_params=params(10),
        name="input_share",
    )(*parts, weight)


def f32(v):
    return v.astype(F32)


def split(v, at):
    n = v.shape[0] // 2
    low, high = v[:n], v[n:]
    return jnp.where(at == 0, low, high), jnp.where(at == 0, high, low)


def unite(mine, other, at):
    return jnp.concatenate([jnp.where(at == 0, mine, other), jnp.where(at == 0, other, mine)], axis=0)


def all_sum(v, masks):
    core, z = masks[0, :1], masks[1, :1]
    mine, other = split(v, core)
    v = mine + lax.ppermute(other, "col", CP)
    n = v.shape[0] // 4
    pieces = [v[i * n : (i + 1) * n] for i in range(4)]

    def piece(k):
        at = (z + k) & 3
        return jnp.where(at < 2, jnp.where(at == 0, pieces[0], pieces[1]), jnp.where(at == 2, pieces[2], pieces[3]))

    v = (piece(0) + zperm(piece(2), 2)) + (zperm(piece(1), 1) + zperm(piece(3), 3))
    v = (v + xperm(v, 2)) + (xperm(v, 1) + xperm(v, 3))
    v = (v + yperm(v, 2)) + (yperm(v, 1) + yperm(v, 3))
    four = [v, zperm(v, 3), zperm(v, 2), zperm(v, 1)]

    def placed(i):
        at = (i - z) & 3
        return jnp.where(at < 2, jnp.where(at == 0, four[0], four[1]), jnp.where(at == 2, four[2], four[3]))

    v = jnp.concatenate([placed(i) for i in range(4)], axis=0)
    return unite(v, cperm(v), core)


def local(out_grad, features, weight, tiles, row_block, col_block, live):
    row, col = lax.axis_index("row"), lax.axis_index("col")
    y, x, z, core = row // NX, row % NX, col // 2, col % 2
    low = low_panels(out_grad)
    one, three, two = zperm(low, 1), zperm(low, 3), zperm(low, 2)
    at = jnp.stack([y, x, z, core]).astype(jnp.int32)
    place = jnp.stack([y, x, core, z]).astype(jnp.int32)
    code = codes(at, row_block, col_block, live, low)
    held, first, second, count, masks = stage(tiles[0, 0], code, place, low)
    low_turned = cperm(low)
    three, two, one = again((three, two, one), held)
    low_all = [low, three, two, one, low_turned, cperm(three), cperm(two), cperm(one)]
    high = high_panels(out_grad, [three])
    one, three = zperm(high, 1), zperm(high, 3)

    ways = ((xperm, 1), (xperm, 3), (yperm, 1), (yperm, 3))

    def swap(buffers):
        return [perm(v, s) for v, (perm, s) in zip(buffers, ways)]

    x_low, send = send_products(first, count, held, low_all)
    high, three, one = again((high, three, one), x_low)
    two = zperm(high, 2)
    got = swap(send)
    keep = keep_products(second, count, held, x_low)
    high_all = [high, three, two, one, cperm(high), cperm(three), cperm(two), cperm(one)]
    x_high, send_high = send_products(first, count, held, high_all)
    got_both = swap(join([keep[1], keep[2], keep[4], keep[5]], got, send_high))
    keep_high = keep_products(second, count, held, x_high)
    turned = [keep_high[1], keep_high[2], keep_high[4], keep_high[5]]
    got_high = swap([(f32(v) + f32(g[8:16])).astype(BF16) for v, g in zip(turned, got_both)])

    def ordered(keep, ones, twos):
        return [keep[0], *ones[:2], *twos[:2], keep[3], *ones[2:], *twos[2:]]

    before = middle(ordered(keep, got, got_both), [])
    sums = middle(ordered(keep_high, got_both, got_high), before)
    parts = [sums[0]] + [yperm(sums[k], k) for k in (1, 2, 3)]
    parts += [sums[4]] + [xperm(sums[4 + k], k) for k in (1, 2, 3)]
    input_grad, wg = input_share(parts, weight), weight_share(parts, features)
    nodes = 1024 * 128
    return input_grad, all_sum(wg, masks) * nodes ** (-0.5)


def solution(mesh):
    return jax.shard_map(
        local,
        mesh=mesh,
        in_specs=(
            P(("row", "col"), None),
            P(("col", "row"), None),
            P(),
            P("row", "col", None, None, None),
            P("row", "col", None),
            P("row", "col", None),
            P("row", "col", None),
        ),
        out_specs=(P(("col", "row"), None), P()),
        check_vma=False,
    )
```

```python
import functools

import jax
import jax.numpy as jnp
from jax import lax
from jax.experimental import pallas as pl
from jax.experimental.pallas import tpu as pltpu
from jax.sharding import PartitionSpec as P

F32, BF16 = jnp.float32, jnp.bfloat16
B = 128
NY = NX = NZ = 4
HALF = 64
UNROLL = 32
KT = 384
VMEM = pl.BlockSpec(memory_space=pltpu.VMEM)
SMEM = pl.BlockSpec(memory_space=pltpu.SMEM)
ANY = pl.BlockSpec(memory_space=pl.ANY)


def params(mib):
    return pltpu.CompilerParams(vmem_limit_bytes=mib * 2**20)


def shaped(shape, dtype=BF16):
    return jax.ShapeDtypeStruct(shape, dtype)


XP = [[(y * NX + x, y * NX + (x + s) % NX) for y in range(NY) for x in range(NX)] for s in range(4)]
YP = [[(y * NX + x, (y + s) % NY * NX + x) for y in range(NY) for x in range(NX)] for s in range(4)]
ZP = [[(z * 2 + c, (z + s) % NZ * 2 + c) for z in range(NZ) for c in range(2)] for s in range(4)]
CP = [(z * 2 + c, z * 2 + 1 - c) for z in range(NZ) for c in range(2)]


def xperm(v, s):
    return lax.ppermute(v, "row", XP[s])


def yperm(v, s):
    return lax.ppermute(v, "row", YP[s])


def zperm(v, s):
    return lax.ppermute(v, "col", ZP[s])


def cperm(v):
    return lax.ppermute(v, "col", CP)


def transposed(x_ref, out_ref):
    for b in range(8):
        out_ref[b] = x_ref[b * B : (b + 1) * B, :].astype(F32).T.astype(BF16)


def low_kernel(x_ref, out_ref):
    transposed(x_ref, out_ref)


def low_panels(out_grad):
    return pl.pallas_call(
        low_kernel,
        grid=(1,),
        in_specs=[pl.BlockSpec((8 * B, B), lambda i: (0, 0))],
        out_specs=pl.BlockSpec((8, B, B), lambda i: (0, 0, 0)),
        out_shape=shaped((8, B, B)),
        compiler_params=params(4),
        name="low_panels",
    )(out_grad)


def codes_kernel(at, row_block, col_block, live, after, code):
    y, x, z, core = (at[i] for i in range(4))
    rb, cb = row_block[...], col_block[...]
    src = rb >> 3
    panel = (((src + core) & 1) << 5) + ((((src >> 1) - z) & 3) << 3) + (rb & 7)
    dest, b = cb >> 3, cb & 7
    rx, ry = (dest - x) & 3, ((dest >> 2) - y) & 3
    in_first = b < 4
    major, minor = jnp.where(in_first, rx, ry), jnp.where(in_first, ry, rx)
    low = minor < 2
    kept = (major == 0) | (low & (major == 1)) | ((minor >= 2) & (major == 3))
    kept_at = minor * 4 + jnp.where(major == 0, 0, 16)
    far = minor * 4 + jnp.where(low, 0, 8)
    near = minor * 4 + jnp.where(major == 1, 0, 24)
    sent_at = jnp.where(major == 2, far, near)
    target = jnp.where(kept, kept_at, sent_at) + (b & 3) + jnp.where(in_first, 0, 32)
    group = jnp.where(live[...] > 0, jnp.where(kept, 1, 0), 2)
    tile = lax.broadcasted_iota(jnp.int32, rb.shape, 2)
    code[...] = (group << 23) + (target << 15) + (panel << 9) + tile


def codes(at, row_block, col_block, live, after):
    return pl.pallas_call(
        codes_kernel,
        in_specs=[SMEM] + [VMEM] * 3 + [ANY],
        out_shape=shaped((1, 1, KT), jnp.int32),
        compiler_params=params(4),
        name="codes",
    )(at, row_block, col_block, live, after)


def high_kernel(x_ref, *refs):
    transposed(x_ref, refs[-1])


def high_panels(out_grad, after):
    return pl.pallas_call(
        high_kernel,
        grid=(1,),
        in_specs=[pl.BlockSpec((8 * B, B), lambda i: (0, 1))] + [ANY] * len(after),
        out_specs=pl.BlockSpec((8, B, B), lambda i: (0, 0, 0)),
        out_shape=shaped((8, B, B)),
        compiler_params=params(4),
        name="high_panels",
    )(out_grad, *after)


def again_kernel(a, b, c, *refs):
    for source, target in zip((a, b, c), refs[-3:]):
        target[...] = source[...]


def again(arrays, after):
    return pl.pallas_call(
        again_kernel,
        in_specs=[VMEM] * 3 + [ANY],
        out_shape=[shaped(a.shape) for a in arrays],
        compiler_params=params(6),
        name="again",
    )(*arrays, after)


def stage_kernel(tiles, code, place, after, held, first, second, count, masks, sem):
    copy = pltpu.make_async_copy(tiles, held, sem)
    copy.start()
    for i in range(2):
        masks[i] = jnp.full((8, 256), place[2 + i], jnp.int32)

    def step(g, counts):
        a, b = counts
        for u in range(8):
            v = code[0, 0, g * 8 + u]
            group = v >> 23
            entry = v & (2**23 - 1)
            first[a] = entry
            second[b] = entry
            a = a + (group == 0).astype(jnp.int32)
            b = b + (group & 1)
        return a, b

    a, b = lax.fori_loop(0, KT // 8, step, (jnp.int32(0), jnp.int32(0)))
    for u in range(UNROLL):
        first[a + u] = HALF * 2**15
        second[b + u] = HALF * 2**15
    count[0] = (a + UNROLL - 1) // UNROLL
    count[1] = (b + UNROLL - 1) // UNROLL
    copy.wait()


def stage(tiles, code, place, after):
    return pl.pallas_call(
        stage_kernel,
        in_specs=[ANY, SMEM, SMEM, ANY],
        out_specs=[VMEM, SMEM, SMEM, SMEM, VMEM],
        out_shape=[
            shaped((KT, B, B)),
            shaped((KT + UNROLL,), jnp.int32),
            shaped((KT + UNROLL,), jnp.int32),
            shaped((2,), jnp.int32),
            shaped((2, 8, 256), jnp.int32),
        ],
        scratch_shapes=[pltpu.SemaphoreType.DMA(())],
        compiler_params=params(16),
        name="stage",
    )(tiles, code, place, after)


def products(which, entries, count, tiles, x, acc):
    acc[...] = jnp.zeros_like(acc)

    def step(g, carry):
        targets, values = [], []
        for u in range(UNROLL):
            v = entries[g * UNROLL + u]
            c = v >> 15
            r = (v >> 9) & 63
            k = v & 511
            targets.append(c)
            values.append(jnp.dot(x[r], tiles[k], preferred_element_type=F32))
        for c, value in zip(targets, values):
            acc[c] += value
        return carry

    lax.fori_loop(0, count[which], step, 0)


def write_out(acc, outs):
    at = 0
    for out in outs:
        n = out.shape[0]
        out[...] = acc[pl.ds(at, n)].astype(BF16)
        at += n


SEND = (16, 16) * 2
KEEP = (16, 8, 8) * 2


def send_kernel(entries, count, tiles, *refs):
    xs, x, outs, acc = refs[:8], refs[8], refs[9:13], refs[13]
    for i in range(8):
        x[i * 8 : (i + 1) * 8] = xs[i][...]
    products(0, entries, count, tiles, x, acc)
    write_out(acc, outs)


def keep_kernel(entries, count, tiles, x, *refs):
    outs, acc = refs[:6], refs[6]
    products(1, entries, count, tiles, x, acc)
    write_out(acc, outs)


ACC = pltpu.VMEM((HALF + 1, B, B), F32)


def send_products(entries, count, tiles, xs):
    out = pl.pallas_call(
        send_kernel,
        in_specs=[SMEM, SMEM, VMEM] + [VMEM] * 8,
        out_specs=[VMEM] * 5,
        out_shape=[shaped((n, B, B)) for n in (64,) + SEND],
        scratch_shapes=[ACC],
        compiler_params=params(12),
        name="send_products",
    )(entries, count, tiles, *xs)
    return out[0], out[1:]


def keep_products(entries, count, tiles, x):
    return pl.pallas_call(
        keep_kernel,
        in_specs=[SMEM, SMEM, VMEM, VMEM],
        out_specs=[VMEM] * 6,
        out_shape=[shaped((n, B, B)) for n in KEEP],
        scratch_shapes=[ACC],
        compiler_params=params(12),
        name="keep_products",
    )(entries, count, tiles, x)


def join_kernel(*refs):
    ins, outs = refs[:12], refs[12:]
    for i in range(4):
        kept, got, sent = ins[i * 3 : i * 3 + 3]
        outs[i][:8] = (kept[...].astype(F32) + got[:8].astype(F32)).astype(BF16)
        outs[i][8:] = sent[...]


def join(keep, received, send):
    ins = []
    for kept, got, sent in zip(keep, received, send):
        ins += [kept, got, sent]
    return pl.pallas_call(
        join_kernel,
        out_shape=[shaped((24, B, B))] * 4,
        compiler_params=params(12),
        name="join",
    )(*ins)


def middle_kernel(*refs):
    received = refs[:10]
    last = len(refs) > 18
    before, outs = (refs[10:18], refs[18:]) if last else ((), refs[10:])
    at, skip = (4, 8) if last else (0, 0)
    if last:
        for i in range(8):
            outs[i][:4] = before[i][...]
    for half in range(2):
        own, rp, rm, sp, sm = received[half * 5 : half * 5 + 5]
        for place in range(4):
            out = outs[half * 4 + place]
            for i in range(4):
                n = place * 4 + i
                if place < 2:
                    s = own[n].astype(F32) + rm[skip + 8 + n].astype(F32) + sp[n].astype(F32)
                else:
                    s = own[n].astype(F32) + rp[skip + n].astype(F32) + sm[n - 8].astype(F32)
                out[at + i] = s.astype(out.dtype)


def middle(received, before):
    n = 8 if before else 4
    dtypes = (F32, BF16, BF16, BF16) * 2
    return pl.pallas_call(
        middle_kernel,
        out_shape=[shaped((n, B, B), t) for t in dtypes],
        compiler_params=params(14),
        name="middle",
    )(*received, *before)


def column_grad(parts, b):
    four = parts[b // 4 :: 2]
    halves = []
    for h in range(2):
        i = h * 4 + b % 4
        s = four[0][i] + four[1][i].astype(F32)
        halves.append(s + four[2][i].astype(F32) + four[3][i].astype(F32))
    return jnp.concatenate(halves, axis=0).astype(BF16)


def weight_kernel(*refs):
    parts, (feat, wg) = refs[:8], refs[8:]
    total = jnp.zeros((256, 256), F32)
    for b in range(8):
        total = total + jnp.dot(
            column_grad(parts, b), feat[b * B : (b + 1) * B, :], preferred_element_type=F32
        )
    wg[...] = total.T


def input_kernel(*refs):
    parts, (weight, ig) = refs[:8], refs[8:]
    for b in range(8):
        ig[b * B : (b + 1) * B, :] = lax.dot_general(
            column_grad(parts, b), weight[...], (((0,), (1,)), ((), ())), preferred_element_type=F32
        ).astype(BF16)


def weight_share(parts, features):
    return pl.pallas_call(
        weight_kernel,
        out_shape=shaped((256, 256), F32),
        compiler_params=params(10),
        name="weight_share",
    )(*parts, features)


def input_share(parts, weight):
    return pl.pallas_call(
        input_kernel,
        out_shape=shaped((8 * B, 256)),
        compiler_params=params(10),
        name="input_share",
    )(*parts, weight)


def f32(v):
    return v.astype(F32)


def split(v, at):
    n = v.shape[0] // 2
    low, high = v[:n], v[n:]
    return jnp.where(at == 0, low, high), jnp.where(at == 0, high, low)


def unite(mine, other, at):
    return jnp.concatenate([jnp.where(at == 0, mine, other), jnp.where(at == 0, other, mine)], axis=0)


def all_sum(v, masks):
    core, z = masks[0, :1], masks[1, :1]
    mine, other = split(v, core)
    v = mine + lax.ppermute(other, "col", CP)
    n = v.shape[0] // 4
    pieces = [v[i * n : (i + 1) * n] for i in range(4)]

    def piece(k):
        at = (z + k) & 3
        return jnp.where(at < 2, jnp.where(at == 0, pieces[0], pieces[1]), jnp.where(at == 2, pieces[2], pieces[3]))

    v = (piece(0) + zperm(piece(2), 2)) + (zperm(piece(1), 1) + zperm(piece(3), 3))
    v = (v + xperm(v, 2)) + (xperm(v, 1) + xperm(v, 3))
    v = (v + yperm(v, 2)) + (yperm(v, 1) + yperm(v, 3))
    four = [v, zperm(v, 3), zperm(v, 2), zperm(v, 1)]

    def placed(i):
        at = (i - z) & 3
        return jnp.where(at < 2, jnp.where(at == 0, four[0], four[1]), jnp.where(at == 2, four[2], four[3]))

    v = jnp.concatenate([placed(i) for i in range(4)], axis=0)
    return unite(v, cperm(v), core)


def local(out_grad, features, weight, tiles, row_block, col_block, live):
    row, col = lax.axis_index("row"), lax.axis_index("col")
    y, x, z, core = row // NX, row % NX, col // 2, col % 2
    low = low_panels(out_grad)
    one, three, two = zperm(low, 1), zperm(low, 3), zperm(low, 2)
    at = jnp.stack([y, x, z, core]).astype(jnp.int32)
    place = jnp.stack([y, x, core, z]).astype(jnp.int32)
    code = codes(at, row_block, col_block, live, low)
    held, first, second, count, masks = stage(pltpu.with_memory_space_constraint(tiles[0, 0], pltpu.HBM), code, place, low)
    low_turned = cperm(low)
    two, three, one = again((two, three, one), held)
    low_all = [low, three, two, one, low_turned, cperm(three), cperm(two), cperm(one)]
    high = high_panels(out_grad, [three])
    one, three = zperm(high, 1), zperm(high, 3)

    ways = ((xperm, 1), (xperm, 3), (yperm, 1), (yperm, 3))

    def swap(buffers):
        return [perm(v, s) for v, (perm, s) in zip(buffers, ways)]

    x_low, send = send_products(first, count, held, low_all)
    high, three, one = again((high, three, one), x_low)
    two = zperm(high, 2)
    got = swap(send)
    keep = keep_products(second, count, held, x_low)
    high_all = [high, three, two, one, cperm(high), cperm(three), cperm(two), cperm(one)]
    x_high, send_high = send_products(first, count, held, high_all)
    got_both = swap(join([keep[1], keep[2], keep[4], keep[5]], got, send_high))
    keep_high = keep_products(second, count, held, x_high)
    turned = [keep_high[1], keep_high[2], keep_high[4], keep_high[5]]
    got_high = swap([(f32(v) + f32(g[8:16])).astype(BF16) for v, g in zip(turned, got_both)])

    def ordered(keep, ones, twos):
        return [keep[0], *ones[:2], *twos[:2], keep[3], *ones[2:], *twos[2:]]

    before = middle(ordered(keep, got, got_both), [])
    sums = middle(ordered(keep_high, got_both, got_high), before)
    parts = [sums[0], sums[4]]
    for k in (1, 3, 2):
        parts += [yperm(sums[k], k), xperm(sums[4 + k], k)]
    input_grad, wg = input_share(parts, weight), weight_share(parts, features)
    nodes = 1024 * 128
    return input_grad, all_sum(wg, masks) * nodes ** (-0.5)


def solution(mesh):
    return jax.shard_map(
        local,
        mesh=mesh,
        in_specs=(
            P(("row", "col"), None),
            P(("col", "row"), None),
            P(),
            P("row", "col", None, None, None),
            P("row", "col", None),
            P("row", "col", None),
            P("row", "col", None),
        ),
        out_specs=(P(("col", "row"), None), P()),
        check_vma=False,
    )
```

```python
import functools

import jax
import jax.numpy as jnp
from jax import lax
from jax.experimental import pallas as pl
from jax.experimental.pallas import tpu as pltpu
from jax.sharding import PartitionSpec as P

F32, BF16 = jnp.float32, jnp.bfloat16
B = 128
NY = NX = NZ = 4
HALF = 64
UNROLL = 32
KT = 384
VMEM = pl.BlockSpec(memory_space=pltpu.VMEM)
SMEM = pl.BlockSpec(memory_space=pltpu.SMEM)
ANY = pl.BlockSpec(memory_space=pl.ANY)


def params(mib):
    return pltpu.CompilerParams(vmem_limit_bytes=mib * 2**20)


def shaped(shape, dtype=BF16):
    return jax.ShapeDtypeStruct(shape, dtype)


XP = [[(y * NX + x, y * NX + (x + s) % NX) for y in range(NY) for x in range(NX)] for s in range(4)]
YP = [[(y * NX + x, (y + s) % NY * NX + x) for y in range(NY) for x in range(NX)] for s in range(4)]
ZP = [[(z * 2 + c, (z + s) % NZ * 2 + c) for z in range(NZ) for c in range(2)] for s in range(4)]
CP = [(z * 2 + c, z * 2 + 1 - c) for z in range(NZ) for c in range(2)]


def xperm(v, s):
    return lax.ppermute(v, "row", XP[s])


def yperm(v, s):
    return lax.ppermute(v, "row", YP[s])


def zperm(v, s):
    return lax.ppermute(v, "col", ZP[s])


def cperm(v):
    return lax.ppermute(v, "col", CP)


def transposed(x_ref, out_ref):
    for b in range(8):
        out_ref[b] = x_ref[b * B : (b + 1) * B, :].astype(F32).T.astype(BF16)


def low_kernel(x_ref, out_ref):
    transposed(x_ref, out_ref)


def low_panels(out_grad):
    return pl.pallas_call(
        low_kernel,
        grid=(1,),
        in_specs=[pl.BlockSpec((8 * B, B), lambda i: (0, 0))],
        out_specs=pl.BlockSpec((8, B, B), lambda i: (0, 0, 0)),
        out_shape=shaped((8, B, B)),
        compiler_params=params(4),
        name="low_panels",
    )(out_grad)


def codes_kernel(at, row_block, col_block, live, after, code):
    y, x, z, core = (at[i] for i in range(4))
    rb, cb = row_block[...], col_block[...]
    src = rb >> 3
    panel = (((src + core) & 1) << 5) + ((((src >> 1) - z) & 3) << 3) + (rb & 7)
    dest, b = cb >> 3, cb & 7
    rx, ry = (dest - x) & 3, ((dest >> 2) - y) & 3
    in_first = b < 4
    major, minor = jnp.where(in_first, rx, ry), jnp.where(in_first, ry, rx)
    low = minor < 2
    kept = (major == 0) | (low & (major == 1)) | ((minor >= 2) & (major == 3))
    kept_at = minor * 4 + jnp.where(major == 0, 0, 16)
    far = minor * 4 + jnp.where(low, 0, 8)
    near = minor * 4 + jnp.where(major == 1, 0, 24)
    sent_at = jnp.where(major == 2, far, near)
    target = jnp.where(kept, kept_at, sent_at) + (b & 3) + jnp.where(in_first, 0, 32)
    group = jnp.where(live[...] > 0, jnp.where(kept, 1, 0), 2)
    tile = lax.broadcasted_iota(jnp.int32, rb.shape, 2)
    code[...] = (group << 23) + (target << 15) + (panel << 9) + tile


def codes(at, row_block, col_block, live, after):
    return pl.pallas_call(
        codes_kernel,
        in_specs=[SMEM] + [VMEM] * 3 + [ANY],
        out_shape=shaped((1, 1, KT), jnp.int32),
        compiler_params=params(4),
        name="codes",
    )(at, row_block, col_block, live, after)


def high_kernel(x_ref, *refs):
    transposed(x_ref, refs[-1])


def high_panels(out_grad, after):
    return pl.pallas_call(
        high_kernel,
        grid=(1,),
        in_specs=[pl.BlockSpec((8 * B, B), lambda i: (0, 1))] + [ANY] * len(after),
        out_specs=pl.BlockSpec((8, B, B), lambda i: (0, 0, 0)),
        out_shape=shaped((8, B, B)),
        compiler_params=params(4),
        name="high_panels",
    )(out_grad, *after)


def again_kernel(a, b, c, *refs):
    for source, target in zip((a, b, c), refs[-3:]):
        target[...] = source[...]


def again(arrays, after):
    return pl.pallas_call(
        again_kernel,
        in_specs=[VMEM] * 3 + [ANY],
        out_shape=[shaped(a.shape) for a in arrays],
        compiler_params=params(6),
        name="again",
    )(*arrays, after)


def stage_kernel(tiles, code, place, after, held, first, second, count, masks, sem):
    copy = pltpu.make_async_copy(tiles, held, sem)
    copy.start()
    for i in range(2):
        masks[i] = jnp.full((8, 256), place[2 + i], jnp.int32)

    def step(g, counts):
        a, b = counts
        for u in range(8):
            v = code[0, 0, g * 8 + u]
            group = v >> 23
            entry = v & (2**23 - 1)
            first[a] = entry
            second[b] = entry
            a = a + (group == 0).astype(jnp.int32)
            b = b + (group & 1)
        return a, b

    a, b = lax.fori_loop(0, KT // 8, step, (jnp.int32(0), jnp.int32(0)))
    for u in range(UNROLL):
        first[a + u] = HALF * 2**15
        second[b + u] = HALF * 2**15
    count[0] = (a + UNROLL - 1) // UNROLL
    count[1] = (b + UNROLL - 1) // UNROLL
    copy.wait()


def stage(tiles, code, place, after):
    return pl.pallas_call(
        stage_kernel,
        in_specs=[ANY, SMEM, SMEM, ANY],
        out_specs=[VMEM, SMEM, SMEM, SMEM, VMEM],
        out_shape=[
            shaped((KT, B, B)),
            shaped((KT + UNROLL,), jnp.int32),
            shaped((KT + UNROLL,), jnp.int32),
            shaped((2,), jnp.int32),
            shaped((2, 8, 256), jnp.int32),
        ],
        scratch_shapes=[pltpu.SemaphoreType.DMA(())],
        compiler_params=params(16),
        name="stage",
    )(tiles, code, place, after)


def products(which, entries, count, tiles, x, acc):
    acc[...] = jnp.zeros_like(acc)

    def step(g, carry):
        targets, values = [], []
        for u in range(UNROLL):
            v = entries[g * UNROLL + u]
            c = v >> 15
            r = (v >> 9) & 63
            k = v & 511
            targets.append(c)
            values.append(jnp.dot(x[r], tiles[k], preferred_element_type=F32))
        for c, value in zip(targets, values):
            acc[c] += value
        return carry

    lax.fori_loop(0, count[which], step, 0)


def write_out(acc, outs):
    at = 0
    for out in outs:
        n = out.shape[0]
        out[...] = acc[pl.ds(at, n)].astype(BF16)
        at += n


SEND = (16, 16) * 2
KEEP = (16, 8, 8) * 2


def send_kernel(entries, count, tiles, *refs):
    xs, x, outs, acc = refs[:8], refs[8], refs[9:13], refs[13]
    for i in range(8):
        x[i * 8 : (i + 1) * 8] = xs[i][...]
    products(0, entries, count, tiles, x, acc)
    write_out(acc, outs)


def keep_kernel(entries, count, tiles, x, *refs):
    outs, acc = refs[:6], refs[6]
    products(1, entries, count, tiles, x, acc)
    write_out(acc, outs)


ACC = pltpu.VMEM((HALF + 1, B, B), F32)


def send_products(entries, count, tiles, xs):
    out = pl.pallas_call(
        send_kernel,
        in_specs=[SMEM, SMEM, VMEM] + [VMEM] * 8,
        out_specs=[VMEM] * 5,
        out_shape=[shaped((n, B, B)) for n in (64,) + SEND],
        scratch_shapes=[ACC],
        compiler_params=params(12),
        name="send_products",
    )(entries, count, tiles, *xs)
    return out[0], out[1:]


def keep_products(entries, count, tiles, x):
    return pl.pallas_call(
        keep_kernel,
        in_specs=[SMEM, SMEM, VMEM, VMEM],
        out_specs=[VMEM] * 6,
        out_shape=[shaped((n, B, B)) for n in KEEP],
        scratch_shapes=[ACC],
        compiler_params=params(12),
        name="keep_products",
    )(entries, count, tiles, x)


def join_kernel(*refs):
    ins, outs = refs[:12], refs[12:]
    for i in range(4):
        kept, got, sent = ins[i * 3 : i * 3 + 3]
        outs[i][:8] = (kept[...].astype(F32) + got[:8].astype(F32)).astype(BF16)
        outs[i][8:] = sent[...]


def join(keep, received, send):
    ins = []
    for kept, got, sent in zip(keep, received, send):
        ins += [kept, got, sent]
    return pl.pallas_call(
        join_kernel,
        out_shape=[shaped((24, B, B))] * 4,
        compiler_params=params(12),
        name="join",
    )(*ins)


def middle_kernel(*refs):
    received = refs[:10]
    last = len(refs) > 18
    before, outs = (refs[10:18], refs[18:]) if last else ((), refs[10:])
    at, skip = (4, 8) if last else (0, 0)
    if last:
        for i in range(8):
            outs[i][:4] = before[i][...]
    for half in range(2):
        own, rp, rm, sp, sm = received[half * 5 : half * 5 + 5]
        for place in range(4):
            out = outs[half * 4 + place]
            for i in range(4):
                n = place * 4 + i
                if place < 2:
                    s = own[n].astype(F32) + rm[skip + 8 + n].astype(F32) + sp[n].astype(F32)
                else:
                    s = own[n].astype(F32) + rp[skip + n].astype(F32) + sm[n - 8].astype(F32)
                out[at + i] = s.astype(out.dtype)


def middle(received, before):
    n = 8 if before else 4
    dtypes = (F32, BF16, BF16, BF16) * 2
    return pl.pallas_call(
        middle_kernel,
        out_shape=[shaped((n, B, B), t) for t in dtypes],
        compiler_params=params(14),
        name="middle",
    )(*received, *before)


def column_grad(parts, b):
    four = parts[b // 4 :: 2]
    halves = []
    for h in range(2):
        i = h * 4 + b % 4
        s = four[0][i] + four[1][i].astype(F32)
        halves.append(s + four[2][i].astype(F32) + four[3][i].astype(F32))
    return jnp.concatenate(halves, axis=0).astype(BF16)


def weight_kernel(*refs):
    parts, (feat, wg) = refs[:8], refs[8:]
    total = jnp.zeros((256, 256), F32)
    for b in range(8):
        total = total + jnp.dot(
            column_grad(parts, b), feat[b * B : (b + 1) * B, :], preferred_element_type=F32
        )
    wg[...] = total.T


def input_kernel(*refs):
    parts, (weight, ig) = refs[:8], refs[8:]
    for b in range(8):
        ig[b * B : (b + 1) * B, :] = lax.dot_general(
            column_grad(parts, b), weight[...], (((0,), (1,)), ((), ())), preferred_element_type=F32
        ).astype(BF16)


def weight_share(parts, features):
    return pl.pallas_call(
        weight_kernel,
        out_shape=shaped((256, 256), F32),
        compiler_params=params(10),
        name="weight_share",
    )(*parts, features)


def input_share(parts, weight):
    return pl.pallas_call(
        input_kernel,
        out_shape=shaped((8 * B, 256)),
        compiler_params=params(10),
        name="input_share",
    )(*parts, weight)


def f32(v):
    return v.astype(F32)


def split(v, at):
    n = v.shape[0] // 2
    low, high = v[:n], v[n:]
    return jnp.where(at == 0, low, high), jnp.where(at == 0, high, low)


def unite(mine, other, at):
    return jnp.concatenate([jnp.where(at == 0, mine, other), jnp.where(at == 0, other, mine)], axis=0)


def all_sum(v, masks):
    core, z = masks[0, :1], masks[1, :1]
    mine, other = split(v, core)
    v = mine + lax.ppermute(other, "col", CP)
    n = v.shape[0] // 4
    pieces = [v[i * n : (i + 1) * n] for i in range(4)]

    def piece(k):
        at = (z + k) & 3
        return jnp.where(at < 2, jnp.where(at == 0, pieces[0], pieces[1]), jnp.where(at == 2, pieces[2], pieces[3]))

    v = (piece(0) + zperm(piece(2), 2)) + (zperm(piece(1), 1) + zperm(piece(3), 3))
    v = (v + xperm(v, 2)) + (xperm(v, 1) + xperm(v, 3))
    v = (v + yperm(v, 2)) + (yperm(v, 1) + yperm(v, 3))
    four = [v, zperm(v, 3), zperm(v, 2), zperm(v, 1)]

    def placed(i):
        at = (i - z) & 3
        return jnp.where(at < 2, jnp.where(at == 0, four[0], four[1]), jnp.where(at == 2, four[2], four[3]))

    v = jnp.concatenate([placed(i) for i in range(4)], axis=0)
    return unite(v, cperm(v), core)


def local(out_grad, features, weight, tiles, row_block, col_block, live):
    row, col = lax.axis_index("row"), lax.axis_index("col")
    y, x, z, core = row // NX, row % NX, col // 2, col % 2
    low = low_panels(pltpu.with_memory_space_constraint(out_grad, pltpu.HBM))
    one, three, two = zperm(low, 1), zperm(low, 3), zperm(low, 2)
    at = jnp.stack([y, x, z, core]).astype(jnp.int32)
    place = jnp.stack([y, x, core, z]).astype(jnp.int32)
    code = codes(at, row_block, col_block, live, low)
    held, first, second, count, masks = stage(pltpu.with_memory_space_constraint(tiles[0, 0], pltpu.HBM), code, place, low)
    low_turned = cperm(low)
    two, three, one = again((two, three, one), held)
    low_all = [low, three, two, one, low_turned, cperm(three), cperm(two), cperm(one)]
    high = high_panels(out_grad, [three])
    one, three = zperm(high, 1), zperm(high, 3)

    ways = ((xperm, 1), (xperm, 3), (yperm, 1), (yperm, 3))

    def swap(buffers):
        return [perm(v, s) for v, (perm, s) in zip(buffers, ways)]

    x_low, send = send_products(first, count, held, low_all)
    high, three, one = again((high, three, one), x_low)
    two = zperm(high, 2)
    got = swap(send)
    keep = keep_products(second, count, held, x_low)
    high_all = [high, three, two, one, cperm(high), cperm(three), cperm(two), cperm(one)]
    x_high, send_high = send_products(first, count, held, high_all)
    got_both = swap(join([keep[1], keep[2], keep[4], keep[5]], got, send_high))
    keep_high = keep_products(second, count, held, x_high)
    turned = [keep_high[1], keep_high[2], keep_high[4], keep_high[5]]
    got_high = swap([(f32(v) + f32(g[8:16])).astype(BF16) for v, g in zip(turned, got_both)])

    def ordered(keep, ones, twos):
        return [keep[0], *ones[:2], *twos[:2], keep[3], *ones[2:], *twos[2:]]

    before = middle(ordered(keep, got, got_both), [])
    sums = middle(ordered(keep_high, got_both, got_high), before)
    parts = [sums[0], sums[4]]
    for k in (1, 3, 2):
        parts += [yperm(sums[k], k), xperm(sums[4 + k], k)]
    input_grad, wg = input_share(parts, weight), weight_share(parts, features)
    nodes = 1024 * 128
    return input_grad, all_sum(wg, masks) * nodes ** (-0.5)


def solution(mesh):
    return jax.shard_map(
        local,
        mesh=mesh,
        in_specs=(
            P(("row", "col"), None),
            P(("col", "row"), None),
            P(),
            P("row", "col", None, None, None),
            P("row", "col", None),
            P("row", "col", None),
            P("row", "col", None),
        ),
        out_specs=(P(("col", "row"), None), P()),
        check_vma=False,
    )
```

```python
import functools

import jax
import jax.numpy as jnp
from jax import lax
from jax.experimental import pallas as pl
from jax.experimental.pallas import tpu as pltpu
from jax.sharding import PartitionSpec as P

F32, BF16 = jnp.float32, jnp.bfloat16
B = 128
NY = NX = NZ = 4
HALF = 64
UNROLL = 32
KT = 384
VMEM = pl.BlockSpec(memory_space=pltpu.VMEM)
SMEM = pl.BlockSpec(memory_space=pltpu.SMEM)
ANY = pl.BlockSpec(memory_space=pl.ANY)


def params(mib):
    return pltpu.CompilerParams(vmem_limit_bytes=mib * 2**20)


def shaped(shape, dtype=BF16):
    return jax.ShapeDtypeStruct(shape, dtype)


XP = [[(y * NX + x, y * NX + (x + s) % NX) for y in range(NY) for x in range(NX)] for s in range(4)]
YP = [[(y * NX + x, (y + s) % NY * NX + x) for y in range(NY) for x in range(NX)] for s in range(4)]
ZP = [[(z * 2 + c, (z + s) % NZ * 2 + c) for z in range(NZ) for c in range(2)] for s in range(4)]
CP = [(z * 2 + c, z * 2 + 1 - c) for z in range(NZ) for c in range(2)]


def xperm(v, s):
    return lax.ppermute(v, "row", XP[s])


def yperm(v, s):
    return lax.ppermute(v, "row", YP[s])


def zperm(v, s):
    return lax.ppermute(v, "col", ZP[s])


def cperm(v):
    return lax.ppermute(v, "col", CP)


def transposed(x_ref, out_ref):
    for b in range(8):
        out_ref[b] = x_ref[b * B : (b + 1) * B, :].astype(F32).T.astype(BF16)


def low_kernel(x_ref, out_ref):
    transposed(x_ref, out_ref)


def low_panels(out_grad):
    return pl.pallas_call(
        low_kernel,
        grid=(1,),
        in_specs=[pl.BlockSpec((8 * B, B), lambda i: (0, 0))],
        out_specs=pl.BlockSpec((8, B, B), lambda i: (0, 0, 0)),
        out_shape=shaped((8, B, B)),
        compiler_params=params(4),
        name="low_panels",
    )(out_grad)


def codes_kernel(at, row_block, col_block, live, after, code):
    y, x, z, core = (at[i] for i in range(4))
    rb, cb = row_block[...], col_block[...]
    src = rb >> 3
    panel = (((src + core) & 1) << 5) + ((((src >> 1) - z) & 3) << 3) + (rb & 7)
    dest, b = cb >> 3, cb & 7
    rx, ry = (dest - x) & 3, ((dest >> 2) - y) & 3
    in_first = b < 4
    major, minor = jnp.where(in_first, rx, ry), jnp.where(in_first, ry, rx)
    low = minor < 2
    kept = (major == 0) | (low & (major == 1)) | ((minor >= 2) & (major == 3))
    kept_at = minor * 4 + jnp.where(major == 0, 0, 16)
    far = minor * 4 + jnp.where(low, 0, 8)
    near = minor * 4 + jnp.where(major == 1, 0, 24)
    sent_at = jnp.where(major == 2, far, near)
    target = jnp.where(kept, kept_at, sent_at) + (b & 3) + jnp.where(in_first, 0, 32)
    group = jnp.where(live[...] > 0, jnp.where(kept, 1, 0), 2)
    tile = lax.broadcasted_iota(jnp.int32, rb.shape, 2)
    code[...] = (group << 23) + (target << 15) + (panel << 9) + tile


def codes(at, row_block, col_block, live, after):
    return pl.pallas_call(
        codes_kernel,
        in_specs=[SMEM] + [VMEM] * 3 + [ANY],
        out_shape=shaped((1, 1, KT), jnp.int32),
        compiler_params=params(4),
        name="codes",
    )(at, row_block, col_block, live, after)


def high_kernel(x_ref, *refs):
    transposed(x_ref, refs[-1])


def high_panels(out_grad, after):
    return pl.pallas_call(
        high_kernel,
        grid=(1,),
        in_specs=[pl.BlockSpec((8 * B, B), lambda i: (0, 1))] + [ANY] * len(after),
        out_specs=pl.BlockSpec((8, B, B), lambda i: (0, 0, 0)),
        out_shape=shaped((8, B, B)),
        compiler_params=params(4),
        name="high_panels",
    )(out_grad, *after)


def again_kernel(a, b, c, *refs):
    for source, target in zip((a, b, c), refs[-3:]):
        target[...] = source[...]


def again(arrays, after):
    return pl.pallas_call(
        again_kernel,
        in_specs=[VMEM] * 3 + [ANY],
        out_shape=[shaped(a.shape) for a in arrays],
        compiler_params=params(6),
        name="again",
    )(*arrays, after)


def stage_kernel(tiles, code, place, after, held, first, second, count, masks, sem):
    copy = pltpu.make_async_copy(tiles, held, sem)
    copy.start()
    for i in range(2):
        masks[i] = jnp.full((8, 256), place[2 + i], jnp.int32)

    def step(g, counts):
        a, b = counts
        for u in range(8):
            v = code[0, 0, g * 8 + u]
            group = v >> 23
            entry = v & (2**23 - 1)
            first[a] = entry
            second[b] = entry
            a = a + (group == 0).astype(jnp.int32)
            b = b + (group & 1)
        return a, b

    a, b = lax.fori_loop(0, KT // 8, step, (jnp.int32(0), jnp.int32(0)))
    for u in range(UNROLL):
        first[a + u] = HALF * 2**15
        second[b + u] = HALF * 2**15
    count[0] = (a + UNROLL - 1) // UNROLL
    count[1] = (b + UNROLL - 1) // UNROLL
    copy.wait()


def stage(tiles, code, place, after):
    return pl.pallas_call(
        stage_kernel,
        in_specs=[ANY, SMEM, SMEM, ANY],
        out_specs=[VMEM, SMEM, SMEM, SMEM, VMEM],
        out_shape=[
            shaped((KT, B, B)),
            shaped((KT + UNROLL,), jnp.int32),
            shaped((KT + UNROLL,), jnp.int32),
            shaped((2,), jnp.int32),
            shaped((2, 8, 256), jnp.int32),
        ],
        scratch_shapes=[pltpu.SemaphoreType.DMA(())],
        compiler_params=params(16),
        name="stage",
    )(tiles, code, place, after)


def products(which, entries, count, tiles, x, acc):
    acc[...] = jnp.zeros_like(acc)

    def step(g, carry):
        targets, values = [], []
        for u in range(UNROLL):
            v = entries[g * UNROLL + u]
            c = v >> 15
            r = (v >> 9) & 63
            k = v & 511
            targets.append(c)
            values.append(jnp.dot(x[r], tiles[k], preferred_element_type=F32))
        for c, value in zip(targets, values):
            acc[c] += value
        return carry

    lax.fori_loop(0, count[which], step, 0)


def write_out(acc, outs):
    at = 0
    for out in outs:
        n = out.shape[0]
        out[...] = acc[pl.ds(at, n)].astype(BF16)
        at += n


SEND = (16, 16) * 2
KEEP = (16, 8, 8) * 2


def send_kernel(entries, count, tiles, *refs):
    xs, x, outs, acc = refs[:8], refs[8], refs[9:13], refs[13]
    for i in range(8):
        x[i * 8 : (i + 1) * 8] = xs[i][...]
    products(0, entries, count, tiles, x, acc)
    write_out(acc, outs)


def keep_kernel(entries, count, tiles, x, *refs):
    outs, acc = refs[:6], refs[6]
    products(1, entries, count, tiles, x, acc)
    write_out(acc, outs)


ACC = pltpu.VMEM((HALF + 1, B, B), F32)


def send_products(entries, count, tiles, xs):
    out = pl.pallas_call(
        send_kernel,
        in_specs=[SMEM, SMEM, VMEM] + [VMEM] * 8,
        out_specs=[VMEM] * 5,
        out_shape=[shaped((n, B, B)) for n in (64,) + SEND],
        scratch_shapes=[ACC],
        compiler_params=params(12),
        name="send_products",
    )(entries, count, tiles, *xs)
    return out[0], out[1:]


def keep_products(entries, count, tiles, x):
    return pl.pallas_call(
        keep_kernel,
        in_specs=[SMEM, SMEM, VMEM, VMEM],
        out_specs=[VMEM] * 6,
        out_shape=[shaped((n, B, B)) for n in KEEP],
        scratch_shapes=[ACC],
        compiler_params=params(12),
        name="keep_products",
    )(entries, count, tiles, x)


def join_kernel(*refs):
    ins, outs = refs[:12], refs[12:]
    for i in range(4):
        kept, got, sent = ins[i * 3 : i * 3 + 3]
        outs[i][:8] = (kept[...].astype(F32) + got[:8].astype(F32)).astype(BF16)
        outs[i][8:] = sent[...]


def join(keep, received, send):
    ins = []
    for kept, got, sent in zip(keep, received, send):
        ins += [kept, got, sent]
    return pl.pallas_call(
        join_kernel,
        out_shape=[shaped((24, B, B))] * 4,
        compiler_params=params(12),
        name="join",
    )(*ins)


def middle_kernel(*refs):
    received = refs[:10]
    last = len(refs) > 18
    before, outs = (refs[10:18], refs[18:]) if last else ((), refs[10:])
    at, skip = (4, 8) if last else (0, 0)
    if last:
        for i in range(8):
            outs[i][:4] = before[i][...]
    for half in range(2):
        own, rp, rm, sp, sm = received[half * 5 : half * 5 + 5]
        for place in range(4):
            out = outs[half * 4 + place]
            for i in range(4):
                n = place * 4 + i
                if place < 2:
                    s = own[n].astype(F32) + rm[skip + 8 + n].astype(F32) + sp[n].astype(F32)
                else:
                    s = own[n].astype(F32) + rp[skip + n].astype(F32) + sm[n - 8].astype(F32)
                out[at + i] = s.astype(out.dtype)


def middle(received, before):
    n = 8 if before else 4
    dtypes = (F32, BF16, BF16, BF16) * 2
    return pl.pallas_call(
        middle_kernel,
        out_shape=[shaped((n, B, B), t) for t in dtypes],
        compiler_params=params(14),
        name="middle",
    )(*received, *before)


def column_grad(parts, b):
    four = parts[b // 4 :: 2]
    halves = []
    for h in range(2):
        i = h * 4 + b % 4
        s = four[0][i] + four[1][i].astype(F32)
        halves.append(s + four[2][i].astype(F32) + four[3][i].astype(F32))
    return jnp.concatenate(halves, axis=0).astype(BF16)


def weight_kernel(*refs):
    parts, (feat, wg) = refs[:8], refs[8:]
    total = jnp.zeros((256, 256), F32)
    for b in range(8):
        total = total + jnp.dot(
            column_grad(parts, b), feat[b * B : (b + 1) * B, :], preferred_element_type=F32
        )
    wg[...] = total.T


def input_kernel(*refs):
    parts, (weight, ig) = refs[:8], refs[8:]
    for b in range(8):
        ig[b * B : (b + 1) * B, :] = lax.dot_general(
            column_grad(parts, b), weight[...], (((0,), (1,)), ((), ())), preferred_element_type=F32
        ).astype(BF16)


def weight_share(parts, features):
    return pl.pallas_call(
        weight_kernel,
        out_shape=shaped((256, 256), F32),
        compiler_params=params(10),
        name="weight_share",
    )(*parts, features)


def input_share(parts, weight):
    return pl.pallas_call(
        input_kernel,
        out_shape=shaped((8 * B, 256)),
        compiler_params=params(10),
        name="input_share",
    )(*parts, weight)


def f32(v):
    return v.astype(F32)


def split(v, at):
    n = v.shape[0] // 2
    low, high = v[:n], v[n:]
    return jnp.where(at == 0, low, high), jnp.where(at == 0, high, low)


def unite(mine, other, at):
    return jnp.concatenate([jnp.where(at == 0, mine, other), jnp.where(at == 0, other, mine)], axis=0)


def all_sum(v, masks):
    core, z = masks[0, :1], masks[1, :1]
    mine, other = split(v, core)
    v = mine + lax.ppermute(other, "col", CP)
    n = v.shape[0] // 4
    pieces = [v[i * n : (i + 1) * n] for i in range(4)]

    def piece(k):
        at = (z + k) & 3
        return jnp.where(at < 2, jnp.where(at == 0, pieces[0], pieces[1]), jnp.where(at == 2, pieces[2], pieces[3]))

    v = (piece(0) + zperm(piece(2), 2)) + (zperm(piece(1), 1) + zperm(piece(3), 3))
    v = (v + xperm(v, 2)) + (xperm(v, 1) + xperm(v, 3))
    v = (v + yperm(v, 2)) + (yperm(v, 1) + yperm(v, 3))
    four = [v, zperm(v, 3), zperm(v, 2), zperm(v, 1)]

    def placed(i):
        at = (i - z) & 3
        return jnp.where(at < 2, jnp.where(at == 0, four[0], four[1]), jnp.where(at == 2, four[2], four[3]))

    v = jnp.concatenate([placed(i) for i in range(4)], axis=0)
    return unite(v, cperm(v), core)


def local(out_grad, features, weight, tiles, row_block, col_block, live):
    row, col = lax.axis_index("row"), lax.axis_index("col")
    y, x, z, core = row // NX, row % NX, col // 2, col % 2
    low = low_panels(out_grad)
    one, three, two = zperm(low, 1), zperm(low, 3), zperm(low, 2)
    at = jnp.stack([y, x, z, core]).astype(jnp.int32)
    place = jnp.stack([y, x, core, z]).astype(jnp.int32)
    code = codes(at, row_block, col_block, live, low)
    held, first, second, count, masks = stage(tiles[0, 0], code, place, low)
    low_turned = cperm(low)
    three, two, one = again((three, two, one), held)
    low_all = [low, three, two, one, low_turned, cperm(three), cperm(two), cperm(one)]
    high = high_panels(out_grad, [three])
    one, three = zperm(high, 1), zperm(high, 3)

    ways = ((xperm, 1), (xperm, 3), (yperm, 1), (yperm, 3))

    def swap(buffers):
        return [perm(v, s) for v, (perm, s) in zip(buffers, ways)]

    x_low, send = send_products(first, count, held, low_all)
    high, three, one = again((high, three, one), x_low)
    two = zperm(high, 2)
    got = swap(send)
    keep = keep_products(second, count, held, x_low)
    high_all = [high, three, two, one, cperm(high), cperm(three), cperm(two), cperm(one)]
    x_high, send_high = send_products(first, count, held, high_all)
    got_both = swap(join([keep[1], keep[2], keep[4], keep[5]], got, send_high))
    keep_high = keep_products(second, count, held, x_high)
    turned = [keep_high[1], keep_high[2], keep_high[4], keep_high[5]]
    got_high = swap([(f32(v) + f32(g[8:16])).astype(BF16) for v, g in zip(turned, got_both)])

    def ordered(keep, ones, twos):
        return [keep[0], *ones[:2], *twos[:2], keep[3], *ones[2:], *twos[2:]]

    before = middle(ordered(keep, got, got_both), [])
    sums = middle(ordered(keep_high, got_both, got_high), before)
    parts = [sums[0], sums[4]]
    for k in (1, 3, 2):
        parts += [yperm(sums[k], k), xperm(sums[4 + k], k)]
    input_grad, wg = input_share(parts, weight), weight_share(parts, features)
    nodes = 1024 * 128
    return input_grad, all_sum(wg, masks) * nodes ** (-0.5)


def solution(mesh):
    return jax.shard_map(
        local,
        mesh=mesh,
        in_specs=(
            P(("row", "col"), None),
            P(("col", "row"), None),
            P(),
            P("row", "col", None, None, None),
            P("row", "col", None),
            P("row", "col", None),
            P("row", "col", None),
        ),
        out_specs=(P(("col", "row"), None), P()),
        check_vma=False,
    )
```
